512 devices in a mesh: seq: 32 (over y, z_hi, core), ch: 16 (over x, z_lo).
Axes of the slice: x: 4, y: 4, z: 16 (z_hi: 4, z_lo: 4; z = z_hi * 4 + z_lo), core: 2. Of those that a mesh axis runs over, the one named last changes fastest.
Arguments:
- tokens: bfloat16 [4096, 8192], P('seq', 'ch'), may hold values from -6 to 6
- gate_weight: bfloat16 [8192, 4096], P('seq', 'ch'), may hold values from -0.0625 to 0.0625
- value_weight: bfloat16 [8192, 4096], P('seq', 'ch'), may hold values from -0.0625 to 0.0625
- out_weight: bfloat16 [4096, 8192], P('ch'), may hold values from -0.125 to 0.125
- filter_spectrum: float32 [2, 4096, 4096], P(None, 'seq', 'ch'), may hold values from -6 to 6
Outputs:
- mixed: bfloat16 [4096, 8192], P('seq', 'ch')
The draws below stay inside these ranges and needn't reach their ends.
All inputs are finite; a program needn't handle non-finite values.
Results may differ from the reference program's by a relative error of at most 0.005.
Values may be sent and summed in bfloat16 or wider, within the bound.
No kernel may reach another device: no remote copies, remote signals or barrier semaphores. Data moves between devices by JAX's collectives and lax.ppermute only.
A program may use at most 64 MiB of HBM per device.

```python
import jax
import jax.numpy as jnp
from jax import lax

D = 8192
C = 4096
TOKENS = 4096


def with_spikes(values, rng, source, target, blocks, factor):
    owner, partner = [(jnp.arange(values.shape[position]) // (values.shape[position] // blocks)).reshape([-1 if axis == position else 1 for axis in range(values.ndim)]) for position in (source, target)]
    chosen = jax.random.permutation(rng, blocks)[partner]
    strong = (owner == chosen) | (owner == (partner + blocks // 2) % blocks)
    return jnp.where(strong, factor * values, values)


def shard_levels(key, shape, pieces, smallest, high):
    level = 1.0
    for dim, shards_of in pieces:
        steps = jax.random.uniform(jax.random.fold_in(jax.random.fold_in(key, 6), dim), (shards_of,), jnp.float32, smallest / len(pieces), high / len(pieces))
        level = level * jnp.repeat(jnp.exp(steps), shape[dim] // shards_of).reshape((-1,) + (1,) * (len(shape) - 1 - dim))
    return level


def bell_draw(stream_key, extent, spread, most, shards=(), kind=jnp.bfloat16):
    loudness = shard_levels(stream_key, extent, shards, -0.22, 0.18) if shards else 1.0
    drawn = jax.random.normal(stream_key, extent, jnp.float32) * spread * loudness
    return jnp.minimum(jnp.maximum(drawn, -most), most).astype(kind)


def gaussian_with(rng, shape, scale, most, pieces, heavy, held_as=jnp.bfloat16):
    array = scale * jax.random.normal(rng, shape, jnp.float32)
    if pieces:
        array = array * shard_levels(rng, shape, pieces, -0.22, 0.18)
    return jnp.clip(with_spikes(array, jax.random.fold_in(rng, 3), *heavy), -most, most).astype(held_as)


def setup_inputs(seed: int = 0) -> dict:
    key_list = jax.random.split(jax.random.key(seed), 6)
    return {
        "tokens": bell_draw(key_list[0], (TOKENS, D), 1.0, 6.0, ((0, 32), (1, 16))),
        "gate_weight": bell_draw(key_list[1], (D, C), D ** -0.5, 0.0625, ((0, 32), (1, 16))),
        "value_weight": bell_draw(key_list[2], (D, C), D ** -0.5, 0.0625, ((0, 32), (1, 16))),
        "out_weight": gaussian_with(key_list[3], (C, D), C ** -0.5, 0.125, ((0, 16),), (0, 1, 16, 2.0)),
        "filter_spectrum": bell_draw(key_list[4], (2, TOKENS, C), 1.0, 6.0, ((1, 32), (2, 16)), jnp.float32),
    }


def reverse_bits(count):
    total_bits = count.bit_length() - 1
    positions = jnp.arange(count, dtype=jnp.int32)
    reversed_codes = jnp.zeros((count,), jnp.int32)
    for bit_level in range(total_bits):
        reversed_codes = reversed_codes | (((positions >> bit_level) & 1) << (total_bits - 1 - bit_level))
    return reversed_codes


def wide_dot(left, right):
    return jnp.dot(left.astype(jnp.float32), right.astype(jnp.float32), preferred_element_type=jnp.float32)


def reference(tokens, gate_weight, value_weight, out_weight, filter_spectrum):
    gate = wide_dot(tokens, gate_weight)
    value = wide_dot(tokens, value_weight)
    spectrum = jnp.fft.fft(value, axis=0)
    order = reverse_bits(TOKENS)
    resp_real = filter_spectrum[0][order]
    resp_imag = filter_spectrum[1][order]
    spec_real = jnp.real(spectrum)
    spec_imag = jnp.imag(spectrum)
    prod_real = spec_real * resp_real - spec_imag * resp_imag
    prod_imag = spec_real * resp_imag + spec_imag * resp_real
    conv = jnp.real(jnp.fft.ifft(lax.complex(prod_real, prod_imag), axis=0)).astype(jnp.float32)
    hidden = (jax.nn.silu(gate) * conv).astype(jnp.bfloat16)
    mixed = wide_dot(hidden, out_weight)
    return mixed.astype(jnp.bfloat16)
```

```python
import math

import jax
import jax.numpy as jnp
import numpy as np
from jax import lax
from jax.sharding import Mesh
from jax.sharding import PartitionSpec as P

SEQ = ("y", "zh", "core")
CH = ("x", "zl")
N1, N2 = 32, 128
TOTAL = N1 * N2
GROUP = 8


def reverse(count):
    bits = count.bit_length() - 1
    return np.array([int(format(i, f"0{bits}b")[::-1], 2) for i in range(count)])


def dft_tables():
    n1, n2 = np.arange(N1), np.arange(N2)
    k1, k2 = reverse(N1), reverse(N2)
    outer = np.exp(-2j * np.pi * np.outer(k1, n1) / N1)
    twist = np.exp(-2j * np.pi * np.outer(k1, n2) / TOTAL)
    inner = np.exp(-2j * np.pi * np.outer(n2, k2) / N2)
    return outer, twist, inner


def f32(values):
    return jnp.asarray(np.ascontiguousarray(values), jnp.float32)


def high(left, right):
    return jnp.dot(left, right, precision=lax.Precision.HIGHEST, preferred_element_type=jnp.float32)


def convolve(signal, response):
    outer, twist, inner = dft_tables()
    rows = N1 * GROUP
    eye = np.eye(GROUP)
    spread = np.kron(outer, eye)
    forward = np.concatenate([spread.real, spread.imag])
    tw = np.repeat(twist, GROUP, axis=0)
    tr, ti = f32(tw.real), f32(tw.imag)
    mixed = high(f32(forward), signal.reshape(rows, N2))
    ar, ai = mixed[:rows], mixed[rows:]
    turned = jnp.concatenate([ar * tr - ai * ti, ar * ti + ai * tr])
    both = high(turned, f32(np.concatenate([inner.real, inner.imag], axis=1)))
    sr = both[:rows, :N2] - both[rows:, N2:]
    si = both[:rows, N2:] + both[rows:, :N2]
    rr, ri = response[0].reshape(rows, N2), response[1].reshape(rows, N2)
    prod = jnp.concatenate([sr * rr - si * ri, sr * ri + si * rr])
    back = inner.T
    both = high(prod, f32(np.concatenate([back.real, -back.imag], axis=1)))
    br = both[:rows, :N2] - both[rows:, N2:]
    bi = both[:rows, N2:] + both[rows:, :N2]
    turned = jnp.concatenate([br * tr + bi * ti, bi * tr - br * ti])
    home = np.conj(spread).T / TOTAL
    conv = high(f32(np.concatenate([home.real, -home.imag], axis=1)), turned)
    return conv.reshape(N1, GROUP, N2)


def gather_over(block, axis):
    count = lax.axis_size(axis)
    return lax.all_to_all(jnp.broadcast_to(block, (count,) + block.shape), axis, 0, 0)


def project(weight, tokens):
    weight = weight.reshape(4, 512, 256)
    return jnp.einsum("xkc,xtk->ct", weight, tokens, preferred_element_type=jnp.float32)


def local(tokens, gate_weight, value_weight, out_weight, filter_spectrum):
    value_rows = lax.all_gather(value_weight, ("y", "core"), axis=0, tiled=True)
    gate_rows = lax.all_gather(gate_weight, ("y", "core"), axis=0, tiled=True)
    swap = [(zh * 4 + zl, zl * 4 + zh) for zh in range(4) for zl in range(4)]
    swapped = lax.ppermute(tokens, ("zh", "zl"), swap)
    near = lax.all_gather(swapped, "zl", axis=0, tiled=True)
    whole = gather_over(near, "x")

    value = project(value_rows, whole).astype(jnp.bfloat16)
    resp = jnp.transpose(filter_spectrum, (2, 0, 1)).reshape(256, 256)
    resp_hi = resp.astype(jnp.bfloat16)
    resp_lo = (resp - resp_hi.astype(jnp.float32)).astype(jnp.bfloat16)
    packet = jnp.concatenate([value, resp_hi, resp_lo], axis=1).reshape(N1, GROUP, 1024)
    packet = lax.all_to_all(packet, SEQ, 0, 0)

    gate = project(gate_rows, whole)
    gate = jnp.transpose(gate.reshape(256, 4, 128), (1, 0, 2))
    gate = lax.psum_scatter(gate, "zh", scatter_dimension=0)

    signal = packet[:, :, :512].reshape(4, 4, 2, GROUP, 4, N2).astype(jnp.float32).sum(axis=1)
    signal = jnp.transpose(signal, (0, 3, 1, 2, 4)).reshape(N1, GROUP, N2)
    resp = packet[:, :, 512:768].astype(jnp.float32) + packet[:, :, 768:].astype(jnp.float32)
    resp = jnp.transpose(resp.reshape(N1, GROUP, 2, N2), (2, 0, 1, 3))
    conv = lax.all_to_all(convolve(signal, resp), SEQ, 0, 0).reshape(256, 128)

    hidden = (jax.nn.silu(gate) * conv).astype(jnp.bfloat16)
    parts = jnp.einsum("ct,cxd->xtd", hidden, out_weight.reshape(256, 4, 2048), preferred_element_type=jnp.float32)
    parts = lax.all_to_all(parts.astype(jnp.bfloat16), "x", 0, 0)
    total = parts.astype(jnp.float32).sum(axis=0).astype(jnp.bfloat16)
    total = jnp.transpose(total.reshape(128, 4, 512), (1, 0, 2))
    total = lax.all_to_all(total, "zl", 0, 0)
    return total.astype(jnp.float32).sum(axis=0).astype(jnp.bfloat16)


def solution(mesh):
    fine = Mesh(mesh.devices.reshape(4, 4, 2, 4, 4), SEQ + CH)
    return jax.shard_map(
        local,
        mesh=fine,
        in_specs=(P(SEQ, CH), P(SEQ, CH), P(SEQ, CH), P(CH, None), P(None, SEQ, CH)),
        out_specs=P(SEQ, CH),
        check_vma=False,
    )
```

```python
import math

import jax
import jax.numpy as jnp
import numpy as np
from jax import lax
from jax.sharding import Mesh
from jax.sharding import PartitionSpec as P

SEQ = ("y", "zh", "core")
CH = ("x", "zl")
N1, N2 = 32, 128
TOTAL = N1 * N2
GROUP = 8


def reverse(count):
    bits = count.bit_length() - 1
    return np.array([int(format(i, f"0{bits}b")[::-1], 2) for i in range(count)])


def dft_tables():
    n1, n2 = np.arange(N1), np.arange(N2)
    k1, k2 = reverse(N1), reverse(N2)
    outer = np.exp(-2j * np.pi * np.outer(k1, n1) / N1)
    twist = np.exp(-2j * np.pi * np.outer(k1, n2) / TOTAL)
    inner = np.exp(-2j * np.pi * np.outer(n2, k2) / N2)
    return outer, twist, inner


def f32(values):
    return jnp.asarray(np.ascontiguousarray(values), jnp.float32)


def high(left, right):
    return jnp.dot(left, right, precision=lax.Precision.HIGHEST, preferred_element_type=jnp.float32)


def convolve(signal, response):
    outer, twist, inner = dft_tables()
    rows = N1 * GROUP
    eye = np.eye(GROUP)
    spread = np.kron(outer, eye)
    forward = np.concatenate([spread.real, spread.imag])
    tw = np.repeat(twist, GROUP, axis=0)
    tr, ti = f32(tw.real), f32(tw.imag)
    mixed = high(f32(forward), signal.reshape(rows, N2))
    ar, ai = mixed[:rows], mixed[rows:]
    turned = jnp.concatenate([ar * tr - ai * ti, ar * ti + ai * tr])
    both = high(turned, f32(np.concatenate([inner.real, inner.imag], axis=1)))
    sr = both[:rows, :N2] - both[rows:, N2:]
    si = both[:rows, N2:] + both[rows:, :N2]
    rr, ri = response[0].reshape(rows, N2), response[1].reshape(rows, N2)
    prod = jnp.concatenate([sr * rr - si * ri, sr * ri + si * rr])
    back = inner.T
    both = high(prod, f32(np.concatenate([back.real, -back.imag], axis=1)))
    br = both[:rows, :N2] - both[rows:, N2:]
    bi = both[:rows, N2:] + both[rows:, :N2]
    turned = jnp.concatenate([br * tr + bi * ti, bi * tr - br * ti])
    home = np.conj(spread).T / TOTAL
    conv = high(f32(np.concatenate([home.real, -home.imag], axis=1)), turned)
    return conv.reshape(N1, GROUP, N2)


def gather_over(block, axis):
    count = lax.axis_size(axis)
    return lax.all_to_all(jnp.broadcast_to(block, (count,) + block.shape), axis, 0, 0)


def after(block, earlier):
    return lax.optimization_barrier((block, earlier))[0]


def project(weight, tokens):
    weight = weight.reshape(4, 512, 256)
    return jnp.einsum("xkc,xtk->ct", weight, tokens, preferred_element_type=jnp.float32)


def exchange(block, axis, apart):
    return lax.ppermute(block, axis, [(i, i ^ apart) for i in range(lax.axis_size(axis))])


def pick(blocks, index):
    return lax.dynamic_index_in_dim(blocks, index, 0, keepdims=False)


def local(tokens, gate_weight, value_weight, out_weight, filter_spectrum):
    column, core, row, high_z = (lax.axis_index(axis) for axis in ("x", "core", "y", "zh"))
    swap = [(zh * 4 + zl, zl * 4 + zh) for zh in range(4) for zl in range(4)]
    swapped = lax.ppermute(tokens, ("zh", "zl"), swap)
    near = gather_over(swapped, "zl").reshape(512, 512)
    whole = gather_over(near, "x")

    def rows_of(weight):
        mine = jnp.stack([exchange(weight, "y", k) if k else weight for k in range(4)])
        mine = jnp.stack([pick(mine, row ^ y) for y in range(4)])
        theirs = exchange(mine, "core", 1)
        return jnp.stack([jnp.where(core == 0, mine, theirs), jnp.where(core == 0, theirs, mine)], axis=1).reshape(2048, 256)

    value_rows = rows_of(after(value_weight, swapped))
    gate_rows = rows_of(after(gate_weight, near))
    whole, value_rows = lax.optimization_barrier((whole, value_rows))

    value = project(value_rows, whole).astype(jnp.bfloat16)
    resp = jnp.transpose(filter_spectrum, (2, 0, 1)).reshape(256, 256).astype(jnp.bfloat16)
    packet = jnp.concatenate([value, resp], axis=1).reshape(N1, GROUP, 768)
    packet = lax.all_to_all(packet, SEQ, 0, 0)

    gate = jnp.transpose(project(gate_rows, whole).reshape(256, 4, 128), (1, 0, 2))
    far = [lax.ppermute(pick(gate, high_z ^ k), ("zh", "core"), [(i, i ^ (2 * k + 1)) for i in range(8)]) for k in (1, 2, 3)]
    gate = pick(gate, high_z) + exchange(sum(far), "core", 1)

    held = after(out_weight, value)

    def share(k):
        return jnp.concatenate([lax.dynamic_slice_in_dim(held, ((column ^ k) * 4 + zl) * 512 + core * 256, 256, 1) for zl in range(4)], axis=1)

    shares = [exchange(share(k), "x", k) if k else share(k) for k in range(4)]

    signal = packet[:, :, :512].reshape(4, 4, 2, GROUP, 4, N2).astype(jnp.float32).sum(axis=1)
    signal = jnp.transpose(signal, (0, 3, 1, 2, 4)).reshape(N1, GROUP, N2)
    resp = packet[:, :, 512:].astype(jnp.float32)
    resp = jnp.transpose(resp.reshape(N1, GROUP, 2, N2), (2, 0, 1, 3))
    conv = lax.all_to_all(convolve(signal, resp), SEQ, 0, 0).reshape(256, 128)
    conv, gate, shares = lax.optimization_barrier((conv, gate, shares))

    hidden = (jax.nn.silu(gate) * conv).astype(jnp.bfloat16)
    hidden = lax.all_to_all(jnp.broadcast_to(hidden, (8, 256, 128)), ("x", "core"), 0, 0).reshape(4, 2, 256, 128)
    total = 0.0
    for k in range(4):
        total = total + jnp.einsum("ect,cd->etd", pick(hidden, column ^ k), shares[k], preferred_element_type=jnp.float32)
    total = jnp.transpose(total.astype(jnp.bfloat16).reshape(2, 128, 4, 256), (2, 0, 1, 3)).reshape(8, 128, 256)
    total = lax.all_to_all(total, ("zl", "core"), 0, 0).reshape(4, 2, 128, 256)
    total = total.astype(jnp.float32).sum(axis=0)
    return jnp.concatenate([total[0], total[1]], axis=1).astype(jnp.bfloat16)


def solution(mesh):
    fine = Mesh(mesh.devices.reshape(4, 4, 2, 4, 4), SEQ + CH)
    return jax.shard_map(
        local,
        mesh=fine,
        in_specs=(P(SEQ, CH), P(SEQ, CH), P(SEQ, CH), P(CH, None), P(None, SEQ, CH)),
        out_specs=P(SEQ, CH),
        check_vma=False,
    )
```

```python
import math

import jax
import jax.numpy as jnp
import numpy as np
from jax import lax
from jax.sharding import Mesh
from jax.sharding import PartitionSpec as P

SEQ = ("y", "zh", "core")
CH = ("x", "zl")
N1, N2 = 32, 128
TOTAL = N1 * N2
GROUP = 8
ARRIVALS = ((0, 3, 2, 1), (3, 1, 0, 2), (1, 3, 2, 0), (2, 1, 0, 3))


def reverse(count):
    bits = count.bit_length() - 1
    return np.array([int(format(i, f"0{bits}b")[::-1], 2) for i in range(count)])


def dft_tables():
    n1, n2 = np.arange(N1), np.arange(N2)
    k1, k2 = reverse(N1), reverse(N2)
    outer = np.exp(-2j * np.pi * np.outer(k1, n1) / N1)
    twist = np.exp(-2j * np.pi * np.outer(k1, n2) / TOTAL)
    inner = np.exp(-2j * np.pi * np.outer(n2, k2) / N2)
    return outer, twist, inner


def f32(values):
    return jnp.asarray(np.ascontiguousarray(values), jnp.float32)


def high(left, right):
    return jnp.dot(left, right, precision=lax.Precision.HIGH, preferred_element_type=jnp.float32)


def convolve(signal, response):
    outer, twist, inner = dft_tables()
    rows = N1 * GROUP
    eye = np.eye(GROUP)
    spread = np.kron(outer, eye)
    forward = np.concatenate([spread.real, spread.imag])
    tw = np.repeat(twist, GROUP, axis=0)
    tr, ti = f32(tw.real), f32(tw.imag)
    mixed = high(f32(forward), signal.reshape(rows, N2))
    ar, ai = mixed[:rows], mixed[rows:]
    turned = jnp.concatenate([ar * tr - ai * ti, ar * ti + ai * tr])
    both = high(turned, f32(np.concatenate([inner.real, inner.imag], axis=1)))
    sr = both[:rows, :N2] - both[rows:, N2:]
    si = both[:rows, N2:] + both[rows:, :N2]
    rr, ri = response[0].reshape(rows, N2), response[1].reshape(rows, N2)
    prod = jnp.concatenate([sr * rr - si * ri, sr * ri + si * rr])
    back = inner.T
    both = high(prod, f32(np.concatenate([back.real, -back.imag], axis=1)))
    br = both[:rows, :N2] - both[rows:, N2:]
    bi = both[:rows, N2:] + both[rows:, :N2]
    turned = jnp.concatenate([br * tr + bi * ti, bi * tr - br * ti])
    home = np.conj(spread).T / TOTAL
    conv = high(f32(np.concatenate([home.real, -home.imag], axis=1)), turned)
    return conv.reshape(N1, GROUP, N2)


def gather_over(block, axis):
    count = lax.axis_size(axis)
    return lax.all_to_all(jnp.broadcast_to(block, (count,) + block.shape), axis, 0, 0)


def after(block, earlier):
    return lax.optimization_barrier((block, earlier))[0]


def exchange(block, axis, apart):
    return lax.ppermute(block, axis, [(i, i ^ apart) for i in range(lax.axis_size(axis))])


def pick(blocks, index):
    return lax.dynamic_index_in_dim(blocks, index, 0, keepdims=False)


def summed(parts):
    total = parts.reshape(4, 4, 2, GROUP, 4, N2).astype(jnp.float32).sum(axis=1)
    return jnp.transpose(total, (0, 3, 1, 2, 4)).reshape(N1, GROUP, N2)


def local(tokens, gate_weight, value_weight, out_weight, filter_spectrum):
    column, core, row = (lax.axis_index(axis) for axis in ("x", "core", "y"))
    swap = [(t * 4 + b, b * 4 + ARRIVALS[b].index(t)) for t in range(4) for b in range(4)]
    swapped = lax.ppermute(tokens, ("zh", "zl"), swap)
    swapped = jnp.where(core == 0, swapped, jnp.concatenate([swapped[:, 256:], swapped[:, :256]], axis=1))
    near = gather_over(swapped, "zl")
    places = jnp.asarray(np.argsort(np.array(ARRIVALS), axis=1), jnp.int32)[lax.axis_index("zh")]
    near = jnp.concatenate([pick(near, places[t]) for t in range(4)])
    both = after(jnp.concatenate([value_weight, gate_weight], axis=1), swapped)
    parts = [both, exchange(both, "y", 1)]
    near, parts[1] = lax.optimization_barrier((near, parts[1]))
    parts += [exchange(parts[1], "y", 3), exchange(both, "y", 3)]
    whole = gather_over(near, "x")

    def by_row(low, high):
        far = [row ^ y for y in range(4)]
        return jnp.stack([jnp.where(k < 2, pick(low, k % 2), pick(high, k % 2)) for k in far])

    low, high = jnp.stack(parts[:2]), jnp.stack(parts[2:])
    mine = by_row(low, high)
    theirs = by_row(exchange(low, "core", 1), exchange(high, "core", 1))
    whole, mine, theirs = lax.optimization_barrier((whole, mine, theirs))

    projected = 0.0
    for rows, part in ((mine, whole[:, :, :256]), (theirs, whole[:, :, 256:])):
        projected = projected + jnp.einsum("xkc,xtk->ct", rows, part, preferred_element_type=jnp.float32)
    projected = projected.astype(jnp.bfloat16)
    value, gate = projected[:256], projected[256:]
    resp = jnp.transpose(filter_spectrum, (2, 0, 1)).reshape(256, 256).astype(jnp.bfloat16)
    packet = jnp.concatenate([value, gate, resp], axis=1).reshape(N1, GROUP, 1280)
    packet = lax.all_to_all(packet, SEQ, 0, 0)

    held = after(out_weight, value)

    def share(k):
        return jnp.concatenate([lax.dynamic_slice_in_dim(held, ((column ^ k) * 4 + zl) * 512 + core * 256, 256, 1) for zl in range(4)], axis=1)

    shares = [exchange(share(k), "x", k) if k else share(k) for k in range(4)]

    signal, gate = (summed(packet[:, :, at : at + 512]) for at in (0, 512))
    resp = packet[:, :, 1024:].astype(jnp.float32)
    resp = jnp.transpose(resp.reshape(N1, GROUP, 2, N2), (2, 0, 1, 3))
    hidden = (jax.nn.silu(gate) * convolve(signal, resp)).astype(jnp.bfloat16)
    hidden = lax.all_to_all(hidden, SEQ, 0, 0).reshape(256, 128)
    hidden, shares = lax.optimization_barrier((hidden, shares))

    hidden = lax.all_to_all(jnp.broadcast_to(hidden, (8, 256, 128)), ("x", "core"), 0, 0).reshape(4, 2, 256, 128)
    total = 0.0
    for k in range(4):
        total = total + jnp.einsum("ect,cd->etd", pick(hidden, column ^ k), shares[k], preferred_element_type=jnp.float32)
    total = jnp.transpose(total.astype(jnp.bfloat16).reshape(2, 128, 4, 256), (2, 0, 1, 3)).reshape(8, 128, 256)
    total = lax.all_to_all(total, ("zl", "core"), 0, 0).reshape(4, 2, 128, 256)
    total = total.astype(jnp.float32).sum(axis=0)
    return jnp.concatenate([total[0], total[1]], axis=1).astype(jnp.bfloat16)


def solution(mesh):
    fine = Mesh(mesh.devices.reshape(4, 4, 2, 4, 4), SEQ + CH)
    return jax.shard_map(
        local,
        mesh=fine,
        in_specs=(P(SEQ, CH), P(SEQ, CH), P(SEQ, CH), P(CH, None), P(None, SEQ, CH)),
        out_specs=P(SEQ, CH),
        check_vma=False,
    )
```

```python
import math

import jax
import jax.numpy as jnp
import numpy as np
from jax import lax
from jax.sharding import Mesh
from jax.sharding import PartitionSpec as P

SEQ = ("y", "zh", "core")
CH = ("x", "zl")
N1, N2 = 32, 128
TOTAL = N1 * N2
GROUP = 8
ARRIVALS = ((0, 3, 2, 1), (3, 1, 0, 2), (1, 3, 2, 0), (2, 1, 0, 3))


def reverse(count):
    bits = count.bit_length() - 1
    return np.array([int(format(i, f"0{bits}b")[::-1], 2) for i in range(count)])


def dft_tables():
    n1, n2 = np.arange(N1), np.arange(N2)
    k1, k2 = reverse(N1), reverse(N2)
    outer = np.exp(-2j * np.pi * np.outer(k1, n1) / N1)
    twist = np.exp(-2j * np.pi * np.outer(k1, n2) / TOTAL)
    inner = np.exp(-2j * np.pi * np.outer(n2, k2) / N2)
    return outer, twist, inner


def f32(values):
    return jnp.asarray(np.ascontiguousarray(values), jnp.float32)


def high(left, right):
    return jnp.dot(left, right, precision=lax.Precision.HIGH, preferred_element_type=jnp.float32)


def convolve(signal, response):
    outer, twist, inner = dft_tables()
    rows = N1 * GROUP
    eye = np.eye(GROUP)
    spread = np.kron(outer, eye)
    forward = np.concatenate([spread.real, spread.imag])
    tw = np.repeat(twist, GROUP, axis=0)
    tr, ti = f32(tw.real), f32(tw.imag)
    mixed = high(f32(forward), signal.reshape(rows, N2))
    ar, ai = mixed[:rows], mixed[rows:]
    turned = jnp.concatenate([ar * tr - ai * ti, ar * ti + ai * tr])
    both = high(turned, f32(np.concatenate([inner.real, inner.imag], axis=1)))
    sr = both[:rows, :N2] - both[rows:, N2:]
    si = both[:rows, N2:] + both[rows:, :N2]
    rr, ri = response[0].reshape(rows, N2), response[1].reshape(rows, N2)
    prod = jnp.concatenate([sr * rr - si * ri, sr * ri + si * rr])
    back = inner.T
    both = high(prod, f32(np.concatenate([back.real, -back.imag], axis=1)))
    br = both[:rows, :N2] - both[rows:, N2:]
    bi = both[:rows, N2:] + both[rows:, :N2]
    turned = jnp.concatenate([br * tr + bi * ti, bi * tr - br * ti])
    home = np.conj(spread).T / TOTAL
    conv = high(f32(np.concatenate([home.real, -home.imag], axis=1)), turned)
    return conv.reshape(N1, GROUP, N2)


def gather_over(block, axis):
    count = lax.axis_size(axis)
    return lax.all_to_all(jnp.broadcast_to(block, (count,) + block.shape), axis, 0, 0)


def after(block, earlier):
    return lax.optimization_barrier((block, earlier))[0]


def exchange(block, axis, apart):
    return lax.ppermute(block, axis, [(i, i ^ apart) for i in range(lax.axis_size(axis))])


def pick(blocks, index):
    return lax.dynamic_index_in_dim(blocks, index, 0, keepdims=False)


def summed(parts):
    total = parts.reshape(4, 4, 2, GROUP, 4, N2).astype(jnp.float32).sum(axis=1)
    return jnp.transpose(total, (0, 3, 1, 2, 4)).reshape(N1, GROUP, N2)


def local(tokens, gate_weight, value_weight, out_weight, filter_spectrum):
    column, core, row = (lax.axis_index(axis) for axis in ("x", "core", "y"))
    swap = [(t * 4 + b, b * 4 + ARRIVALS[b].index(t)) for t in range(4) for b in range(4)]
    swapped = lax.ppermute(tokens, ("zh", "zl"), swap)
    swapped = jnp.where(core == 0, swapped, jnp.concatenate([swapped[:, 256:], swapped[:, :256]], axis=1))
    near = gather_over(swapped, "zl")
    places = jnp.asarray(np.argsort(np.array(ARRIVALS), axis=1), jnp.int32)[lax.axis_index("zh")]
    near = jnp.concatenate([pick(near, places[t]) for t in range(4)])
    both = after(jnp.concatenate([value_weight, gate_weight], axis=1), swapped)
    parts = [both, exchange(both, "y", 1)]
    near, parts[1] = lax.optimization_barrier((near, parts[1]))
    parts += [exchange(parts[1], "y", 3), exchange(both, "y", 3)]
    whole = gather_over(near, "x")

    def by_row(low, high):
        far = [row ^ y for y in range(4)]
        return jnp.stack([jnp.where(k < 2, pick(low, k % 2), pick(high, k % 2)) for k in far])

    low, high = jnp.stack(parts[:2]), jnp.stack(parts[2:])
    mine = by_row(low, high)
    theirs = by_row(exchange(low, "core", 1), exchange(high, "core", 1))
    whole, mine, theirs = lax.optimization_barrier((whole, mine, theirs))

    projected = 0.0
    for rows, part in ((mine, whole[:, :, :256]), (theirs, whole[:, :, 256:])):
        projected = projected + jnp.einsum("xkc,xtk->ct", rows, part, preferred_element_type=jnp.float32)
    projected = projected.astype(jnp.bfloat16)
    value, gate = projected[:256], projected[256:]
    resp = jnp.transpose(filter_spectrum, (2, 0, 1)).reshape(256, 256).astype(jnp.bfloat16)
    packet = jnp.concatenate([value, gate, resp], axis=1).reshape(N1, GROUP, 1280)
    packet = lax.all_to_all(packet, SEQ, 0, 0)

    held = after(out_weight, value)
    own = lax.dynamic_slice_in_dim(held, column * 2048, 2048, 1)
    half = {k: exchange(lax.dynamic_slice(held, (core * 128, (column ^ k) * 2048), (128, 2048)), "x", k) for k in (1, 2, 3)}
    other = {k: exchange(half[k], "core", 1) for k in (1, 2, 3)}

    signal, gate = (summed(packet[:, :, at : at + 512]) for at in (0, 512))
    resp = packet[:, :, 1024:].astype(jnp.float32)
    resp = jnp.transpose(resp.reshape(N1, GROUP, 2, N2), (2, 0, 1, 3))
    hidden = (jax.nn.silu(gate) * convolve(signal, resp)).astype(jnp.bfloat16)
    hidden = lax.all_to_all(hidden, SEQ, 0, 0).reshape(256, 128)
    hidden, other[1], half[3], half[2] = lax.optimization_barrier((hidden, other[1], half[3], half[2]))

    hidden = gather_over(hidden, "x")
    total = jnp.einsum("ct,cd->td", pick(hidden, column), own, preferred_element_type=jnp.float32)
    for k in (1, 3, 2):
        rows = pick(hidden, column ^ k).reshape(2, 128, 128)
        for part, weight in ((core, half[k]), (1 - core, other[k])):
            total = total + jnp.einsum("ct,cd->td", pick(rows, part), weight, preferred_element_type=jnp.float32)
    total = jnp.transpose(total.astype(jnp.bfloat16).reshape(128, 4, 512), (1, 0, 2))
    total = lax.all_to_all(total, "zl", 0, 0)
    return total.astype(jnp.float32).sum(axis=0).astype(jnp.bfloat16)


def solution(mesh):
    fine = Mesh(mesh.devices.reshape(4, 4, 2, 4, 4), SEQ + CH)
    return jax.shard_map(
        local,
        mesh=fine,
        in_specs=(P(SEQ, CH), P(SEQ, CH), P(SEQ, CH), P(CH, None), P(None, SEQ, CH)),
        out_specs=P(SEQ, CH),
        check_vma=False,
    )
```

```python
import math

import jax
import jax.numpy as jnp
import numpy as np
from jax import lax
from jax.sharding import Mesh
from jax.sharding import PartitionSpec as P

SEQ = ("y", "zh", "core")
CH = ("x", "zl")
N1, N2 = 32, 128
TOTAL = N1 * N2
GROUP = 8
ARRIVALS = ((0, 3, 2, 1), (3, 1, 0, 2), (1, 3, 2, 0), (2, 1, 0, 3))


def reverse(count):
    bits = count.bit_length() - 1
    return np.array([int(format(i, f"0{bits}b")[::-1], 2) for i in range(count)])


def dft_tables():
    n1, n2 = np.arange(N1), np.arange(N2)
    k1, k2 = reverse(N1), reverse(N2)
    outer = np.exp(-2j * np.pi * np.outer(k1, n1) / N1)
    twist = np.exp(-2j * np.pi * np.outer(k1, n2) / TOTAL)
    inner = np.exp(-2j * np.pi * np.outer(n2, k2) / N2)
    return outer, twist, inner


def f32(values):
    return jnp.asarray(np.ascontiguousarray(values), jnp.float32)


def high(left, right):
    return jnp.dot(left, right, precision=lax.Precision.HIGH, preferred_element_type=jnp.float32)


def convolve(signal, response):
    outer, twist, inner = dft_tables()
    rows = N1 * GROUP
    eye = np.eye(GROUP)
    spread = np.kron(outer, eye)
    forward = np.concatenate([spread.real, spread.imag])
    tw = np.repeat(twist, GROUP, axis=0)
    tr, ti = f32(tw.real), f32(tw.imag)
    mixed = high(f32(forward), signal.reshape(rows, N2))
    ar, ai = mixed[:rows], mixed[rows:]
    turned = jnp.concatenate([ar * tr - ai * ti, ar * ti + ai * tr])
    both = high(turned, f32(np.concatenate([inner.real, inner.imag], axis=1)))
    sr = both[:rows, :N2] - both[rows:, N2:]
    si = both[:rows, N2:] + both[rows:, :N2]
    rr, ri = response[0].reshape(rows, N2), response[1].reshape(rows, N2)
    prod = jnp.concatenate([sr * rr - si * ri, sr * ri + si * rr])
    back = inner.T
    both = high(prod, f32(np.concatenate([back.real, -back.imag], axis=1)))
    br = both[:rows, :N2] - both[rows:, N2:]
    bi = both[:rows, N2:] + both[rows:, :N2]
    turned = jnp.concatenate([br * tr + bi * ti, bi * tr - br * ti])
    home = np.conj(spread).T / TOTAL
    conv = high(f32(np.concatenate([home.real, -home.imag], axis=1)), turned)
    return conv.reshape(N1, GROUP, N2)


def gather_over(block, axis):
    count = lax.axis_size(axis)
    return lax.all_to_all(jnp.broadcast_to(block, (count,) + block.shape), axis, 0, 0)


def after(block, earlier):
    return lax.optimization_barrier((block, earlier))[0]


def choose(values, index):
    chosen = jnp.int32(values[0])
    for at, value in enumerate(values[1:], 1):
        chosen = jnp.where(index == at, jnp.int32(value), chosen)
    return chosen


def exchange(block, axis, apart):
    return lax.ppermute(block, axis, [(i, i ^ apart) for i in range(lax.axis_size(axis))])


def pick(blocks, index):
    return lax.dynamic_index_in_dim(blocks, index, 0, keepdims=False)


def summed(parts):
    total = parts.reshape(4, 4, 2, GROUP, 4, N2).astype(jnp.float32).sum(axis=1)
    return jnp.transpose(total, (0, 3, 1, 2, 4)).reshape(N1, GROUP, N2)


def local(tokens, gate_weight, value_weight, out_weight, filter_spectrum):
    column, core, row = (lax.axis_index(axis) for axis in ("x", "core", "y"))
    swap = [(t * 4 + b, b * 4 + ARRIVALS[b].index(t)) for t in range(4) for b in range(4)]
    swapped = lax.ppermute(tokens, ("zh", "zl"), swap)
    swapped = jnp.where(core == 0, swapped, jnp.concatenate([swapped[:, 256:], swapped[:, :256]], axis=1))
    near = lax.all_gather(swapped, "zl")
    high_z = lax.axis_index("zh")
    near = jnp.concatenate([pick(near, choose([order.index(t) for order in ARRIVALS], high_z)) for t in range(4)])
    both = jnp.concatenate([value_weight, gate_weight], axis=1)
    parts = [both, exchange(both, "y", 1)]
    near, parts[1] = lax.optimization_barrier((near, parts[1]))
    parts += [exchange(parts[1], "y", 3), exchange(both, "y", 3)]
    whole = gather_over(near, "x")

    def by_row(low, high):
        far = [row ^ y for y in range(4)]
        return jnp.stack([jnp.where(k < 2, pick(low, k % 2), pick(high, k % 2)) for k in far])

    low, high = jnp.stack(parts[:2]), jnp.stack(parts[2:])
    mine = by_row(low, high)
    theirs = by_row(exchange(low, "core", 1), exchange(high, "core", 1))
    whole, mine, theirs = lax.optimization_barrier((whole, mine, theirs))

    projected = 0.0
    for rows, part in ((mine, whole[:, :, :256]), (theirs, whole[:, :, 256:])):
        projected = projected + jnp.einsum("xkc,xtk->ct", rows, part, preferred_element_type=jnp.float32)
    projected = projected.astype(jnp.bfloat16)
    value, gate = projected[:256], projected[256:]
    resp = jnp.transpose(filter_spectrum, (2, 0, 1)).reshape(256, 256).astype(jnp.bfloat16)
    packet = jnp.concatenate([value, gate, resp], axis=1).reshape(N1, GROUP, 1280)
    packet = lax.all_to_all(packet, SEQ, 0, 0)

    held = after(out_weight, value)
    own = lax.dynamic_slice_in_dim(held, column * 2048, 2048, 1)
    half = {k: exchange(lax.dynamic_slice(held, (core * 128, (column ^ k) * 2048), (128, 2048)), "x", k) for k in (1, 2, 3)}
    other = {k: exchange(half[k], "core", 1) for k in (1, 2, 3)}

    signal, gate = (summed(packet[:, :, at : at + 512]) for at in (0, 512))
    resp = packet[:, :, 1024:].astype(jnp.float32)
    resp = jnp.transpose(resp.reshape(N1, GROUP, 2, N2), (2, 0, 1, 3))
    hidden = (jax.nn.silu(gate) * convolve(signal, resp)).astype(jnp.bfloat16)
    hidden = lax.all_to_all(hidden, SEQ, 0, 0).reshape(256, 128)
    hidden, other[1], half[3], half[2] = lax.optimization_barrier((hidden, other[1], half[3], half[2]))

    hidden = gather_over(hidden, "x")
    total = jnp.einsum("ct,cd->td", pick(hidden, column), own, preferred_element_type=jnp.float32)
    for k in (1, 3, 2):
        rows = pick(hidden, column ^ k).reshape(2, 128, 128)
        for part, weight in ((core, half[k]), (1 - core, other[k])):
            total = total + jnp.einsum("ct,cd->td", pick(rows, part), weight, preferred_element_type=jnp.float32)
    total = jnp.transpose(total.astype(jnp.bfloat16).reshape(128, 4, 512), (1, 0, 2))
    total = lax.all_to_all(total, "zl", 0, 0)
    return total.astype(jnp.float32).sum(axis=0).astype(jnp.bfloat16)


def solution(mesh):
    fine = Mesh(mesh.devices.reshape(4, 4, 2, 4, 4), SEQ + CH)
    return jax.shard_map(
        local,
        mesh=fine,
        in_specs=(P(SEQ, CH), P(SEQ, CH), P(SEQ, CH), P(CH, None), P(None, SEQ, CH)),
        out_specs=P(SEQ, CH),
        check_vma=False,
    )
```

```python
import math

import jax
import jax.numpy as jnp
import numpy as np
from jax import lax
from jax.sharding import Mesh
from jax.sharding import PartitionSpec as P

SEQ = ("y", "zh", "core")
SPREAD = ("zh", "y", "core")
CH = ("x", "zl")
N1, N2 = 32, 128
TOTAL = N1 * N2
GROUP = 8
ARRIVALS = ((0, 3, 2, 1), (3, 1, 0, 2), (1, 3, 2, 0), (2, 1, 0, 3))


def reverse(count):
    bits = count.bit_length() - 1
    return np.array([int(format(i, f"0{bits}b")[::-1], 2) for i in range(count)])


def dft_tables():
    n1, n2 = np.array([y * 8 + zh * 2 + core for zh in range(4) for y in range(4) for core in range(2)]), np.arange(N2)
    k1, k2 = reverse(N1)[n1], reverse(N2)
    outer = np.exp(-2j * np.pi * np.outer(k1, n1) / N1)
    twist = np.exp(-2j * np.pi * np.outer(k1, n2) / TOTAL)
    inner = np.exp(-2j * np.pi * np.outer(n2, k2) / N2)
    return outer, twist, inner


def f32(values):
    return jnp.asarray(np.ascontiguousarray(values), jnp.float32)


def high(left, right):
    return jnp.dot(left, right, precision=lax.Precision.HIGH, preferred_element_type=jnp.float32)


def convolve(signal, response):
    outer, twist, inner = dft_tables()
    rows = N1 * GROUP
    eye = np.eye(GROUP)
    spread = np.kron(outer, eye)
    forward = np.concatenate([spread.real, spread.imag])
    tw = np.repeat(twist, GROUP, axis=0)
    tr, ti = f32(tw.real), f32(tw.imag)
    mixed = high(f32(forward), signal.reshape(rows, N2))
    ar, ai = mixed[:rows], mixed[rows:]
    turned = jnp.concatenate([ar * tr - ai * ti, ar * ti + ai * tr])
    both = high(turned, f32(np.concatenate([inner.real, inner.imag], axis=1)))
    sr = both[:rows, :N2] - both[rows:, N2:]
    si = both[:rows, N2:] + both[rows:, :N2]
    rr, ri = response[0].reshape(rows, N2), response[1].reshape(rows, N2)
    prod = jnp.concatenate([sr * rr - si * ri, sr * ri + si * rr])
    back = inner.T
    both = high(prod, f32(np.concatenate([back.real, -back.imag], axis=1)))
    br = both[:rows, :N2] - both[rows:, N2:]
    bi = both[:rows, N2:] + both[rows:, :N2]
    turned = jnp.concatenate([br * tr + bi * ti, bi * tr - br * ti])
    home = np.conj(spread).T / TOTAL
    conv = high(f32(np.concatenate([home.real, -home.imag], axis=1)), turned)
    return conv.reshape(N1, GROUP, N2)


def gather_over(block, axis):
    count = lax.axis_size(axis)
    return lax.all_to_all(jnp.broadcast_to(block, (count,) + block.shape), axis, 0, 0)


def after(block, earlier):
    return lax.optimization_barrier((block, earlier))[0]


def choose(values, index):
    chosen = jnp.int32(values[0])
    for at, value in enumerate(values[1:], 1):
        chosen = jnp.where(index == at, jnp.int32(value), chosen)
    return chosen


def exchange(block, axis, apart):
    return lax.ppermute(block, axis, [(i, i ^ apart) for i in range(lax.axis_size(axis))])


def pick(blocks, index):
    return lax.dynamic_index_in_dim(blocks, index, 0, keepdims=False)


def summed(parts):
    total = parts.reshape(4, 4, 2, GROUP, 4, N2).astype(jnp.float32).sum(axis=0)
    return jnp.transpose(total, (3, 0, 1, 2, 4)).reshape(N1, GROUP, N2)


def local(tokens, gate_weight, value_weight, out_weight, filter_spectrum):
    column, core, row = (lax.axis_index(axis) for axis in ("x", "core", "y"))
    swap = [(t * 4 + b, b * 4 + ARRIVALS[b].index(t)) for t in range(4) for b in range(4)]
    swapped = lax.ppermute(tokens, ("zh", "zl"), swap)
    swapped = jnp.where(core == 0, swapped, jnp.concatenate([swapped[:, 256:], swapped[:, :256]], axis=1))
    near = lax.all_gather(swapped, "zl")
    high_z = lax.axis_index("zh")
    near = jnp.concatenate([pick(near, choose([order.index(t) for order in ARRIVALS], high_z)) for t in range(4)])
    both = jnp.concatenate([value_weight, gate_weight], axis=1)
    parts = [both, exchange(both, "y", 1)]
    near, parts[1] = lax.optimization_barrier((near, parts[1]))
    parts += [exchange(parts[1], "y", 3), exchange(both, "y", 3)]
    whole = gather_over(near, "x")

    def by_row(low, high):
        far = [row ^ y for y in range(4)]
        return jnp.stack([jnp.where(k < 2, pick(low, k % 2), pick(high, k % 2)) for k in far])

    low, high = jnp.stack(parts[:2]), jnp.stack(parts[2:])
    mine = by_row(low, high)
    theirs = by_row(exchange(low, "core", 1), exchange(high, "core", 1))
    whole, mine, theirs = lax.optimization_barrier((whole, mine, theirs))

    projected = 0.0
    for rows, part in ((mine, whole[:, :, :256]), (theirs, whole[:, :, 256:])):
        projected = projected + jnp.einsum("xkc,xtk->ct", rows, part, preferred_element_type=jnp.float32)
    projected = projected.astype(jnp.bfloat16)
    value, gate = projected[:256], projected[256:]
    resp = jnp.transpose(filter_spectrum, (2, 0, 1)).reshape(256, 256).astype(jnp.bfloat16)
    packet = jnp.concatenate([value, gate, resp], axis=1).reshape(N1, GROUP, 1280)
    packet = lax.all_to_all(packet, SPREAD, 0, 0)

    held = after(out_weight, value)
    own = jnp.concatenate([lax.dynamic_slice(held, (part * 128, column * 2048), (128, 2048)) for part in (core, 1 - core)])
    half = {k: exchange(lax.dynamic_slice(held, (core * 128, (column ^ k) * 2048), (128, 2048)), "x", k) for k in (1, 2, 3)}
    other = {k: exchange(half[k], "core", 1) for k in (1, 2, 3)}

    signal, gate = (summed(packet[:, :, at : at + 512]) for at in (0, 512))
    resp = packet[:, :, 1024:].astype(jnp.float32)
    resp = jnp.transpose(resp.reshape(N1, GROUP, 2, N2), (2, 0, 1, 3))
    hidden = (jax.nn.silu(gate) * convolve(signal, resp)).astype(jnp.bfloat16)
    hidden = lax.all_to_all(hidden, SPREAD, 0, 0).reshape(256, 128)
    hidden, other[1], half[3], half[2] = lax.optimization_barrier((hidden, other[1], half[3], half[2]))

    hidden = jnp.where(core == 0, hidden, jnp.concatenate([hidden[128:], hidden[:128]]))
    hidden = gather_over(hidden, "x")
    total = jnp.einsum("ct,cd->td", pick(hidden, column), own, preferred_element_type=jnp.float32)
    for k in (1, 3, 2):
        rows = pick(hidden, column ^ k)
        for part, weight in ((rows[:128], half[k]), (rows[128:], other[k])):
            total = total + jnp.einsum("ct,cd->td", part, weight, preferred_element_type=jnp.float32)
    total = jnp.transpose(total.astype(jnp.bfloat16).reshape(128, 4, 512), (1, 0, 2))
    total = lax.all_to_all(total, "zl", 0, 0)
    return total.astype(jnp.float32).sum(axis=0).astype(jnp.bfloat16)


def solution(mesh):
    fine = Mesh(mesh.devices.reshape(4, 4, 2, 4, 4), SEQ + CH)
    return jax.shard_map(
        local,
        mesh=fine,
        in_specs=(P(SEQ, CH), P(SEQ, CH), P(SEQ, CH), P(CH, None), P(None, SEQ, CH)),
        out_specs=P(SEQ, CH),
        check_vma=False,
    )
```

```python
import math

import jax
import jax.numpy as jnp
import numpy as np
from jax import lax
from jax.sharding import Mesh
from jax.sharding import PartitionSpec as P

SEQ = ("y", "zh", "core")
SPREAD = ("zh", "y", "core")
CH = ("x", "zl")
N1, N2 = 32, 128
TOTAL = N1 * N2
GROUP = 8
ARRIVALS = ((0, 3, 1, 2), (0, 1, 2, 3), (0, 1, 2, 3), (1, 2, 0, 3))


def reverse(count):
    bits = count.bit_length() - 1
    return np.array([int(format(i, f"0{bits}b")[::-1], 2) for i in range(count)])


def dft_tables():
    n1, n2 = np.array([y * 8 + zh * 2 + core for zh in range(4) for y in range(4) for core in range(2)]), np.arange(N2)
    k1, k2 = reverse(N1)[n1], reverse(N2)
    outer = np.exp(-2j * np.pi * np.outer(k1, n1) / N1)
    twist = np.exp(-2j * np.pi * np.outer(k1, n2) / TOTAL)
    inner = np.exp(-2j * np.pi * np.outer(n2, k2) / N2)
    return outer, twist, inner


def f32(values):
    return jnp.asarray(np.ascontiguousarray(values), jnp.float32)


def high(left, right):
    return jnp.dot(left, right, precision=lax.Precision.HIGH, preferred_element_type=jnp.float32)


def convolve(signal, response):
    outer, twist, inner = dft_tables()
    rows = N1 * GROUP
    eye = np.eye(GROUP)
    spread = np.kron(outer, eye)
    forward = np.concatenate([spread.real, spread.imag])
    tw = np.repeat(twist, GROUP, axis=0)
    tr, ti = f32(tw.real), f32(tw.imag)
    mixed = high(f32(forward), signal.reshape(rows, N2))
    ar, ai = mixed[:rows], mixed[rows:]
    turned = jnp.concatenate([ar * tr - ai * ti, ar * ti + ai * tr])
    both = high(turned, f32(np.concatenate([inner.real, inner.imag], axis=1)))
    sr = both[:rows, :N2] - both[rows:, N2:]
    si = both[:rows, N2:] + both[rows:, :N2]
    rr, ri = response[0].reshape(rows, N2), response[1].reshape(rows, N2)
    prod = jnp.concatenate([sr * rr - si * ri, sr * ri + si * rr])
    back = inner.T
    both = high(prod, f32(np.concatenate([back.real, -back.imag], axis=1)))
    br = both[:rows, :N2] - both[rows:, N2:]
    bi = both[:rows, N2:] + both[rows:, :N2]
    turned = jnp.concatenate([br * tr + bi * ti, bi * tr - br * ti])
    home = np.conj(spread).T / TOTAL
    conv = high(f32(np.concatenate([home.real, -home.imag], axis=1)), turned)
    return conv.reshape(N1, GROUP, N2)


def gather_over(block, axis):
    count = lax.axis_size(axis)
    return lax.all_to_all(jnp.broadcast_to(block, (count,) + block.shape), axis, 0, 0)


def after(block, earlier):
    return lax.optimization_barrier((block, earlier))[0]


def choose(values, index):
    chosen = jnp.int32(values[0])
    for at, value in enumerate(values[1:], 1):
        chosen = jnp.where(index == at, jnp.int32(value), chosen)
    return chosen


def exchange(block, axis, apart):
    return lax.ppermute(block, axis, [(i, i ^ apart) for i in range(lax.axis_size(axis))])


def pick(blocks, index):
    return lax.dynamic_index_in_dim(blocks, index, 0, keepdims=False)


def summed(parts):
    total = parts.reshape(4, 4, 2, GROUP, 4, N2).astype(jnp.float32).sum(axis=0)
    return jnp.transpose(total, (3, 0, 1, 2, 4)).reshape(N1, GROUP, N2)


def local(tokens, gate_weight, value_weight, out_weight, filter_spectrum):
    column, core, row = (lax.axis_index(axis) for axis in ("x", "core", "y"))
    swap = [(t * 4 + b, b * 4 + ARRIVALS[b].index(t)) for t in range(4) for b in range(4)]
    swapped = lax.ppermute(tokens, ("zh", "zl"), swap)
    swapped = jnp.where(core == 0, swapped, jnp.concatenate([swapped[:, 256:], swapped[:, :256]], axis=1))
    near = lax.all_gather(swapped, "zl")
    high_z = lax.axis_index("zh")
    near = jnp.concatenate([pick(near, choose([order.index(t) for order in ARRIVALS], high_z)) for t in range(4)])
    both = jnp.concatenate([value_weight, gate_weight], axis=1)
    parts = [both, exchange(both, "y", 1)]
    near, parts[1] = lax.optimization_barrier((near, parts[1]))
    parts += [exchange(parts[1], "y", 3), exchange(both, "y", 3)]
    whole = gather_over(near, "x")

    def by_row(low, high):
        far = [row ^ y for y in range(4)]
        return jnp.stack([jnp.where(k < 2, pick(low, k % 2), pick(high, k % 2)) for k in far])

    low, high = jnp.stack(parts[:2]), jnp.stack(parts[2:])
    mine = by_row(low, high)
    theirs = by_row(exchange(low, "core", 1), exchange(high, "core", 1))
    whole, mine, theirs = lax.optimization_barrier((whole, mine, theirs))

    projected = 0.0
    for rows, part in ((mine, whole[:, :, :256]), (theirs, whole[:, :, 256:])):
        projected = projected + jnp.einsum("xkc,xtk->ct", rows, part, preferred_element_type=jnp.float32)
    projected = projected.astype(jnp.bfloat16)
    value, gate = projected[:256], projected[256:]
    resp = jnp.transpose(filter_spectrum, (2, 0, 1)).reshape(256, 256).astype(jnp.bfloat16)
    packet = jnp.concatenate([value, gate, resp], axis=1).reshape(N1, GROUP, 1280)
    packet = lax.all_to_all(packet, SPREAD, 0, 0)

    held = after(out_weight, value)
    own = jnp.concatenate([lax.dynamic_slice(held, (part * 128, column * 2048), (128, 2048)) for part in (core, 1 - core)])
    half = {k: exchange(lax.dynamic_slice(held, (core * 128, (column ^ k) * 2048), (128, 2048)), "x", k) for k in (1, 2, 3)}
    other = {k: exchange(half[k], "core", 1) for k in (1, 2, 3)}

    signal, gate = (summed(packet[:, :, at : at + 512]) for at in (0, 512))
    resp = packet[:, :, 1024:].astype(jnp.float32)
    resp = jnp.transpose(resp.reshape(N1, GROUP, 2, N2), (2, 0, 1, 3))
    hidden = (jax.nn.silu(gate) * convolve(signal, resp)).astype(jnp.bfloat16)
    hidden = lax.all_to_all(hidden, SPREAD, 0, 0).reshape(256, 128)
    hidden, other[1], half[3], half[2] = lax.optimization_barrier((hidden, other[1], half[3], half[2]))

    hidden = jnp.where(core == 0, hidden, jnp.concatenate([hidden[128:], hidden[:128]]))
    hidden = gather_over(hidden, "x")
    total = jnp.einsum("ct,cd->td", pick(hidden, column), own, preferred_element_type=jnp.float32)
    for k in (1, 3, 2):
        rows = pick(hidden, column ^ k)
        for part, weight in ((rows[:128], half[k]), (rows[128:], other[k])):
            total = total + jnp.einsum("ct,cd->td", part, weight, preferred_element_type=jnp.float32)
    total = jnp.transpose(total.astype(jnp.bfloat16).reshape(128, 4, 512), (1, 0, 2))
    total = lax.all_to_all(total, "zl", 0, 0)
    return total.astype(jnp.float32).sum(axis=0).astype(jnp.bfloat16)


def solution(mesh):
    fine = Mesh(mesh.devices.reshape(4, 4, 2, 4, 4), SEQ + CH)
    return jax.shard_map(
        local,
        mesh=fine,
        in_specs=(P(SEQ, CH), P(SEQ, CH), P(SEQ, CH), P(CH, None), P(None, SEQ, CH)),
        out_specs=P(SEQ, CH),
        check_vma=False,
    )
```

```python
import math

import jax
import jax.numpy as jnp
import numpy as np
from jax import lax
from jax.sharding import Mesh
from jax.sharding import PartitionSpec as P

SEQ = ("y", "zh", "core")
SPREAD = ("zh", "y", "core")
CH = ("x", "zl")
N1, N2 = 32, 128
TOTAL = N1 * N2
GROUP = 8
ARRIVALS = ((0, 3, 1, 2), (0, 1, 2, 3), (0, 1, 2, 3), (1, 2, 0, 3))


def reverse(count):
    bits = count.bit_length() - 1
    return np.array([int(format(i, f"0{bits}b")[::-1], 2) for i in range(count)])


def dft_tables():
    n1, n2 = np.array([y * 8 + zh * 2 + core for zh in range(4) for y in range(4) for core in range(2)]), np.arange(N2)
    k1, k2 = reverse(N1)[n1], reverse(N2)
    outer = np.exp(-2j * np.pi * np.outer(k1, n1) / N1)
    twist = np.exp(-2j * np.pi * np.outer(k1, n2) / TOTAL)
    inner = np.exp(-2j * np.pi * np.outer(n2, k2) / N2)
    return outer, twist, inner


def f32(values):
    return jnp.asarray(np.ascontiguousarray(values), jnp.float32)


def high(left, right):
    return jnp.dot(left, right, precision=lax.Precision.HIGH, preferred_element_type=jnp.float32)


def convolve(signal, response):
    outer, twist, inner = dft_tables()
    rows = N1 * GROUP
    eye = np.eye(GROUP)
    spread = np.kron(outer, eye)
    forward = np.concatenate([spread.real, spread.imag])
    tw = np.repeat(twist, GROUP, axis=0)
    tr, ti = f32(tw.real), f32(tw.imag)
    mixed = high(f32(forward), signal.reshape(rows, N2))
    ar, ai = mixed[:rows], mixed[rows:]
    turned = jnp.concatenate([ar * tr - ai * ti, ar * ti + ai * tr])
    both = high(turned, f32(np.concatenate([inner.real, inner.imag], axis=1)))
    sr = both[:rows, :N2] - both[rows:, N2:]
    si = both[:rows, N2:] + both[rows:, :N2]
    rr, ri = response[0].reshape(rows, N2), response[1].reshape(rows, N2)
    prod = jnp.concatenate([sr * rr - si * ri, sr * ri + si * rr])
    back = inner.T
    both = high(prod, f32(np.concatenate([back.real, -back.imag], axis=1)))
    br = both[:rows, :N2] - both[rows:, N2:]
    bi = both[:rows, N2:] + both[rows:, :N2]
    turned = jnp.concatenate([br * tr + bi * ti, bi * tr - br * ti])
    home = np.conj(spread).T / TOTAL
    conv = high(f32(np.concatenate([home.real, -home.imag], axis=1)), turned)
    return conv.reshape(N1, GROUP, N2)


def gather_over(block, axis):
    count = lax.axis_size(axis)
    return lax.all_to_all(jnp.broadcast_to(block, (count,) + block.shape), axis, 0, 0)


def after(block, earlier):
    return lax.optimization_barrier((block, earlier))[0]


def choose(values, index):
    chosen = jnp.int32(values[0])
    for at, value in enumerate(values[1:], 1):
        chosen = jnp.where(index == at, jnp.int32(value), chosen)
    return chosen


def exchange(block, axis, apart):
    return lax.ppermute(block, axis, [(i, i ^ apart) for i in range(lax.axis_size(axis))])


def pick(blocks, index):
    return lax.dynamic_index_in_dim(blocks, index, 0, keepdims=False)


def summed(parts):
    total = parts.reshape(4, 4, 2, GROUP, 4, N2).astype(jnp.float32).sum(axis=0)
    return jnp.transpose(total, (3, 0, 1, 2, 4)).reshape(N1, GROUP, N2)


def local(tokens, gate_weight, value_weight, out_weight, filter_spectrum):
    column, core, row = (lax.axis_index(axis) for axis in ("x", "core", "y"))
    swap = [(t * 4 + b, b * 4 + ARRIVALS[b].index(t)) for t in range(4) for b in range(4)]
    swapped = lax.ppermute(tokens, ("zh", "zl"), swap)
    swapped = jnp.where(core == 0, swapped, jnp.concatenate([swapped[:, 256:], swapped[:, :256]], axis=1))
    near = lax.all_gather(swapped, "zl")
    high_z = lax.axis_index("zh")
    near = jnp.concatenate([pick(near, choose([order.index(t) for order in ARRIVALS], high_z)) for t in range(4)])
    both = jnp.concatenate([value_weight, gate_weight], axis=1)
    parts = [both, exchange(both, "y", 1)]
    near, parts[1] = lax.optimization_barrier((near, parts[1]))
    parts += [exchange(parts[1], "y", 3), exchange(both, "y", 3)]
    whole = gather_over(near, "x")

    def by_row(low, high):
        far = [row ^ y for y in range(4)]
        return jnp.stack([jnp.where(k < 2, pick(low, k % 2), pick(high, k % 2)) for k in far])

    low, high = jnp.stack(parts[:2]), jnp.stack(parts[2:])
    mine = by_row(low, high)
    theirs = by_row(exchange(low, "core", 1), exchange(high, "core", 1))
    whole, mine, theirs = lax.optimization_barrier((whole, mine, theirs))

    projected = 0.0
    for rows, part in ((mine, whole[:, :, :256]), (theirs, whole[:, :, 256:])):
        projected = projected + jnp.einsum("xkc,xtk->ct", rows, part, preferred_element_type=jnp.float32)
    projected = projected.astype(jnp.bfloat16)
    value, gate = projected[:256], projected[256:]
    resp = jnp.transpose(filter_spectrum, (2, 0, 1)).reshape(256, 256).astype(jnp.bfloat16)
    packet = jnp.concatenate([value, gate, resp], axis=1).reshape(N1, GROUP, 1280)
    packet = lax.all_to_all(packet, SPREAD, 0, 0)

    held = after(out_weight, value)
    own = lax.dynamic_slice_in_dim(held, column * 2048, 2048, 1)
    half = {k: exchange(lax.dynamic_slice(held, (core * 128, (column ^ k) * 2048), (128, 2048)), "x", k) for k in (1, 2, 3)}
    other = {k: exchange(half[k], "core", 1) for k in (1, 2, 3)}

    signal, gate = (summed(packet[:, :, at : at + 512]) for at in (0, 512))
    resp = packet[:, :, 1024:].astype(jnp.float32)
    resp = jnp.transpose(resp.reshape(N1, GROUP, 2, N2), (2, 0, 1, 3))
    hidden = (jax.nn.silu(gate) * convolve(signal, resp)).astype(jnp.bfloat16)
    hidden = lax.all_to_all(hidden, SPREAD, 0, 0).reshape(256, 128)
    hidden, other[1], half[3], half[2] = lax.optimization_barrier((hidden, other[1], half[3], half[2]))

    total = jnp.einsum("ct,cd->td", hidden, own, preferred_element_type=jnp.float32)
    hidden = jnp.where(core == 0, hidden, jnp.concatenate([hidden[128:], hidden[:128]]))
    hidden = gather_over(hidden, "x")
    for k in (1, 3, 2):
        rows = pick(hidden, column ^ k)
        for part, weight in ((rows[:128], half[k]), (rows[128:], other[k])):
            total = total + jnp.einsum("ct,cd->td", part, weight, preferred_element_type=jnp.float32)
    total = jnp.transpose(total.astype(jnp.bfloat16).reshape(128, 4, 512), (1, 0, 2))
    total = lax.all_to_all(total, "zl", 0, 0)
    return total.astype(jnp.float32).sum(axis=0).astype(jnp.bfloat16)


def solution(mesh):
    fine = Mesh(mesh.devices.reshape(4, 4, 2, 4, 4), SEQ + CH)
    return jax.shard_map(
        local,
        mesh=fine,
        in_specs=(P(SEQ, CH), P(SEQ, CH), P(SEQ, CH), P(CH, None), P(None, SEQ, CH)),
        out_specs=P(SEQ, CH),
        check_vma=False,
    )
```

```python
import math

import jax
import jax.numpy as jnp
import numpy as np
from jax import lax
from jax.sharding import Mesh
from jax.sharding import PartitionSpec as P

SEQ = ("y", "zh", "core")
SPREAD = ("zh", "y", "core")
CH = ("x", "zl")
N1, N2 = 32, 128
TOTAL = N1 * N2
GROUP = 8
ARRIVALS = ((0, 3, 1, 2), (3, 1, 0, 2), (0, 1, 2, 3), (1, 2, 0, 3))


def reverse(count):
    bits = count.bit_length() - 1
    return np.array([int(format(i, f"0{bits}b")[::-1], 2) for i in range(count)])


def dft_tables():
    n1, n2 = np.array([y * 8 + zh * 2 + core for zh in range(4) for y in range(4) for core in range(2)]), np.arange(N2)
    k1, k2 = reverse(N1)[n1], reverse(N2)
    outer = np.exp(-2j * np.pi * np.outer(k1, n1) / N1)
    twist = np.exp(-2j * np.pi * np.outer(k1, n2) / TOTAL)
    inner = np.exp(-2j * np.pi * np.outer(n2, k2) / N2)
    return outer, twist, inner


def f32(values):
    return jnp.asarray(np.ascontiguousarray(values), jnp.float32)


def high(left, right):
    return jnp.dot(left, right, precision=lax.Precision.HIGH, preferred_element_type=jnp.float32)


def convolve(signal, response):
    outer, twist, inner = dft_tables()
    rows = N1 * GROUP
    eye = np.eye(GROUP)
    spread = np.kron(outer, eye)
    forward = np.concatenate([spread.real, spread.imag])
    tw = np.repeat(twist, GROUP, axis=0)
    tr, ti = f32(tw.real), f32(tw.imag)
    mixed = high(f32(forward), signal.reshape(rows, N2))
    ar, ai = mixed[:rows], mixed[rows:]
    turned = jnp.concatenate([ar * tr - ai * ti, ar * ti + ai * tr])
    both = high(turned, f32(np.concatenate([inner.real, inner.imag], axis=1)))
    sr = both[:rows, :N2] - both[rows:, N2:]
    si = both[:rows, N2:] + both[rows:, :N2]
    rr, ri = response[0].reshape(rows, N2), response[1].reshape(rows, N2)
    prod = jnp.concatenate([sr * rr - si * ri, sr * ri + si * rr])
    back = inner.T
    both = high(prod, f32(np.concatenate([back.real, -back.imag], axis=1)))
    br = both[:rows, :N2] - both[rows:, N2:]
    bi = both[:rows, N2:] + both[rows:, :N2]
    turned = jnp.concatenate([br * tr + bi * ti, bi * tr - br * ti])
    home = np.conj(spread).T / TOTAL
    conv = high(f32(np.concatenate([home.real, -home.imag], axis=1)), turned)
    return conv.reshape(N1, GROUP, N2)


def gather_over(block, axis):
    count = lax.axis_size(axis)
    return lax.all_to_all(jnp.broadcast_to(block, (count,) + block.shape), axis, 0, 0)


def after(block, earlier):
    return lax.optimization_barrier((block, earlier))[0]


def choose(values, index):
    chosen = jnp.int32(values[0])
    for at, value in enumerate(values[1:], 1):
        chosen = jnp.where(index == at, jnp.int32(value), chosen)
    return chosen


def exchange(block, axis, apart):
    return lax.ppermute(block, axis, [(i, i ^ apart) for i in range(lax.axis_size(axis))])


def pick(blocks, index):
    return lax.dynamic_index_in_dim(blocks, index, 0, keepdims=False)


def summed(parts):
    total = parts.reshape(4, 4, 2, GROUP, 4, N2).astype(jnp.float32).sum(axis=0)
    return jnp.transpose(total, (3, 0, 1, 2, 4)).reshape(N1, GROUP, N2)


def local(tokens, gate_weight, value_weight, out_weight, filter_spectrum):
    column, core, row = (lax.axis_index(axis) for axis in ("x", "core", "y"))
    swap = [(t * 4 + b, b * 4 + ARRIVALS[b].index(t)) for t in range(4) for b in range(4)]
    swapped = lax.ppermute(tokens, ("zh", "zl"), swap)
    swapped = jnp.where(core == 0, swapped, jnp.concatenate([swapped[:, 256:], swapped[:, :256]], axis=1))
    near = lax.all_gather(swapped, "zl")
    high_z = lax.axis_index("zh")
    near = jnp.concatenate([pick(near, choose([order.index(t) for order in ARRIVALS], high_z)) for t in range(4)])
    both = jnp.concatenate([value_weight, gate_weight], axis=1)
    parts = [both, exchange(both, "y", 1)]
    near, parts[1] = lax.optimization_barrier((near, parts[1]))
    parts += [exchange(parts[1], "y", 3), exchange(both, "y", 3)]
    whole = gather_over(near, "x")

    def by_row(low, high):
        far = [row ^ y for y in range(4)]
        return jnp.stack([jnp.where(k < 2, pick(low, k % 2), pick(high, k % 2)) for k in far])

    low, high = jnp.stack(parts[:2]), jnp.stack(parts[2:])
    mine = by_row(low, high)
    theirs = by_row(exchange(low, "core", 1), exchange(high, "core", 1))
    whole, mine, theirs = lax.optimization_barrier((whole, mine, theirs))

    projected = 0.0
    for rows, part in ((mine, whole[:, :, :256]), (theirs, whole[:, :, 256:])):
        projected = projected + jnp.einsum("xkc,xtk->ct", rows, part, preferred_element_type=jnp.float32)
    projected = projected.astype(jnp.bfloat16)
    value, gate = projected[:256], projected[256:]
    resp = jnp.transpose(filter_spectrum, (2, 0, 1)).reshape(256, 256).astype(jnp.bfloat16)
    packet = jnp.concatenate([value, gate, resp], axis=1).reshape(N1, GROUP, 1280)
    packet = lax.all_to_all(packet, SPREAD, 0, 0)

    held = after(out_weight, value)
    own = lax.dynamic_slice_in_dim(held, column * 2048, 2048, 1)
    half = {k: exchange(lax.dynamic_slice(held, (core * 128, (column ^ k) * 2048), (128, 2048)), "x", k) for k in (1, 2, 3)}
    other = {k: exchange(half[k], "core", 1) for k in (1, 2, 3)}

    signal, gate = (summed(packet[:, :, at : at + 512]) for at in (0, 512))
    resp = packet[:, :, 1024:].astype(jnp.float32)
    resp = jnp.transpose(resp.reshape(N1, GROUP, 2, N2), (2, 0, 1, 3))
    hidden = (jax.nn.silu(gate) * convolve(signal, resp)).astype(jnp.bfloat16)
    hidden = lax.all_to_all(hidden, SPREAD, 0, 0).reshape(256, 128)
    hidden, other[1], half[3], half[2] = lax.optimization_barrier((hidden, other[1], half[3], half[2]))

    total = jnp.einsum("ct,cd->td", hidden, own, preferred_element_type=jnp.float32)
    hidden = jnp.where(core == 0, hidden, jnp.concatenate([hidden[128:], hidden[:128]]))
    hidden = gather_over(hidden, "x")
    for k in (1, 3, 2):
        rows = pick(hidden, column ^ k)
        for part, weight in ((rows[:128], half[k]), (rows[128:], other[k])):
            total = total + jnp.einsum("ct,cd->td", part, weight, preferred_element_type=jnp.float32)
    total = jnp.transpose(total.astype(jnp.bfloat16).reshape(128, 4, 512), (1, 0, 2))
    total = lax.all_to_all(total, "zl", 0, 0)
    return total.astype(jnp.float32).sum(axis=0).astype(jnp.bfloat16)


def solution(mesh):
    fine = Mesh(mesh.devices.reshape(4, 4, 2, 4, 4), SEQ + CH)
    return jax.shard_map(
        local,
        mesh=fine,
        in_specs=(P(SEQ, CH), P(SEQ, CH), P(SEQ, CH), P(CH, None), P(None, SEQ, CH)),
        out_specs=P(SEQ, CH),
        check_vma=False,
    )
```
